512 devices in a mesh: rep: 32 (over x_lo, y, core), fsdp: 16 (over z, x_hi).
Axes of the slice: x: 4 (x_hi: 2, x_lo: 2; x = x_hi * 2 + x_lo), y: 8, z: 8, core: 2. Of those that a mesh axis runs over, the one named last changes fastest.
Arguments:
- inputs: bfloat16 [32, 4096, 4096], P('rep', 'fsdp'), may hold values from -6 to 6
- up_grads: bfloat16 [32, 4096, 512], P('rep', 'fsdp'), may hold values from -0.09375 to 0.09375
- momentum: float32 [32, 4096, 512], P('rep', 'fsdp'), may hold values from -6 to 6
- selected: int32 [32, 64, 8, 32], P('rep', 'fsdp'), may hold values from 0 to 4095, as said below
Outputs:
- new_momentum: float32 [32, 4096, 512], P('rep', 'fsdp')
- update: bfloat16 [4096, 512], P('fsdp')
The draws below stay inside these ranges and needn't reach their ends.
Inputs may be any that keep to these rules, and one draw needn't show every extreme that they name: `selected`: each list holds 32 different row-major positions of a 64 x 64 block, chosen by each replica on its own (for example from earlier magnitudes), so other replicas cannot derive them; they differ between replicas and blocks.
All inputs are finite; a program needn't handle non-finite values.
Results may differ from the reference program's by a relative error of at most 0.017.
Values may be sent and summed in bfloat16 or wider, within the bound.
A program may use at most 128 MiB of HBM per device.

```python
import jax
import jax.numpy as jnp
from jax import lax

D = 4096
SPAN = 64
TOPK = 32
COLS = 512
TOK_DEV = 256
BLOCKS = 8
TOKENS = 4096
REPLICAS = 32
N_FSDP = 16


def draw_selected(key, part):
    key = jax.random.fold_in(key, 7)
    list_count = REPLICAS * (D // SPAN) * BLOCKS
    key_list = jax.random.split(key, list_count)

    def one_list(single):
        return jax.random.permutation(single, SPAN * SPAN)[:TOPK]
    picked_lists = jax.vmap(one_list)(key_list)
    return picked_lists.reshape(REPLICAS, D // SPAN, BLOCKS, TOPK).astype(jnp.int32)


def strengthened(entries, key, source, target, parts, factor):
    def block_of(axis_at):
        return (jnp.arange(entries.shape[axis_at]) // (entries.shape[axis_at] // parts)).reshape((-1,) + (1,) * (entries.ndim - 1 - axis_at))

    first = jax.random.permutation(key, parts)[block_of(target)]
    other_side = (block_of(target) + parts // 2) % parts
    return jnp.where((block_of(source) == first) | (block_of(source) == other_side), factor * entries, entries)


def levels(stream_key, dims, shards, low, largest):
    factor_of, own = 1.0, jax.random.fold_in(stream_key, 6)
    for axis_at, shards_of in shards:
        steps = jnp.exp(jax.random.uniform(jax.random.fold_in(own, axis_at), (shards_of,), jnp.float32, low / len(shards), largest / len(shards)))
        factor_of = factor_of * jnp.repeat(steps, dims[axis_at] // shards_of).reshape([-1 if axis == axis_at else 1 for axis in range(len(dims))])
    return factor_of


def normal_values(own_key, extent, spread, bound, pieces=(), held_as=jnp.bfloat16):
    result = jax.random.normal(own_key, extent, jnp.float32) * spread
    if len(pieces) > 0:
        result = levels(own_key, extent, pieces, -0.22, 0.18) * result
    return jnp.clip(result, min=-bound, max=bound).astype(held_as)


def noise_with(stream_key, extent, width, bound, cuts, heavy, held_as=jnp.bfloat16):
    result = width * jax.random.normal(stream_key, extent, jnp.float32)
    if cuts:
        result = result * levels(stream_key, extent, cuts, -0.22, 0.18)
    return jnp.clip(strengthened(result, jax.random.fold_in(stream_key, 3), *heavy), -bound, bound).astype(held_as)


def setup_inputs(seed: int = 0) -> dict:
    key_of = jax.random.split(jax.random.key(seed), 5)
    return {
        "inputs": noise_with(key_of[0], (REPLICAS, TOKENS, D), 1.0, 6.0, ((0, 32), (1, 16)), (1, 2, 16, 2.0)),
        "up_grads": normal_values(key_of[1], (REPLICAS, TOKENS, COLS), TOKENS ** -0.5, 0.09375, ((0, 32), (1, 16))),
        "momentum": normal_values(key_of[2], (REPLICAS, D, COLS), 1.0, 6.0, ((0, 32), (1, 16)), jnp.float32),
        "selected": draw_selected(jax.random.fold_in(key_of[4], 71), 0),
    }


highest = lax.Precision.HIGHEST
momentum_decay = 0.999
epsilon = 1e-06

def cosine_basis():
    freq = jnp.arange(SPAN, dtype=jnp.float32)[:, None]
    sample = jnp.arange(SPAN, dtype=jnp.float32)[None, :]
    cosines = jnp.cos(jnp.pi * (2.0 * sample + 1.0) * freq / (2.0 * SPAN))
    factor = jnp.where(freq == 0, jnp.sqrt(1.0 / SPAN), jnp.sqrt(2.0 / SPAN))
    return cosines * factor

def split_spans(field):
    return field.reshape(field.shape[0] // SPAN, SPAN, field.shape[1] // SPAN, SPAN).transpose(0, 2, 1, 3)

def join_spans(blocks):
    return blocks.transpose(0, 2, 1, 3).reshape(blocks.shape[0] * SPAN, blocks.shape[1] * SPAN)

def forward_cosine(blocks, cosines):
    partly = jnp.einsum('ui,rcij->rcuj', cosines, blocks, precision=highest)
    return jnp.einsum('rcuj,vj->rcuv', partly, cosines, precision=highest)

def inverse_cosine(coefs, cosines):
    partly = jnp.einsum('ui,rcuv->rciv', cosines, coefs, precision=highest)
    return jnp.einsum('rciv,vj->rcij', partly, cosines, precision=highest)

def densify(values, indices):
    rows_b = indices.shape[-3]
    cols_b = indices.shape[-2]
    offsets = (jnp.arange(rows_b * cols_b, dtype=jnp.int32) * (SPAN * SPAN)).reshape(rows_b, cols_b, 1)
    flat_index = (indices + offsets).reshape(-1)
    dense_grid = jnp.zeros((rows_b * cols_b * SPAN * SPAN,), jnp.float32).at[flat_index].add(values.reshape(-1))
    return dense_grid.reshape(rows_b, cols_b, SPAN, SPAN)

def reference(inputs, up_grads, momentum, selected):
    cosines = cosine_basis()

    def one_replica(packed):
        tokens, signals, moment, chosen = packed
        tok_f = tokens.reshape(N_FSDP, TOK_DEV, D).astype(jnp.float32)
        sig_f = signals.reshape(N_FSDP, TOK_DEV, COLS).astype(jnp.float32)
        partials = jnp.einsum('ntd,ntc->ndc', tok_f, sig_f).astype(jnp.bfloat16)
        partials = lax.optimization_barrier(partials)
        gradient = lax.optimization_barrier(jnp.sum(partials.astype(jnp.float32), axis=0))
        stepped = momentum_decay * moment + gradient
        blocks = split_spans(stepped)
        coefs = forward_cosine(blocks, cosines)
        picked = jnp.take_along_axis(coefs.reshape(blocks.shape[0], blocks.shape[1], SPAN * SPAN), chosen, axis=2)
        own_part = inverse_cosine(densify(picked, chosen), cosines)
        return (stepped - join_spans(own_part), picked)
    new_momentum, picked = lax.map(one_replica, (inputs, up_grads, momentum, selected))
    summed = densify(picked, selected)
    decoded = inverse_cosine(summed, cosines)
    magnitude = jnp.sqrt(lax.optimization_barrier(jnp.mean(decoded * decoded, axis=(2, 3), keepdims=True)) + epsilon)
    update = join_spans(decoded / magnitude).astype(jnp.bfloat16)
    return (new_momentum, update)
```

```python
import jax
import jax.numpy as jnp
import numpy as np
from jax import lax
from jax.experimental import pallas as pl
from jax.experimental.pallas import tpu as pltpu
from jax.sharding import PartitionSpec as P

MESH = pl.DeviceIdType.MESH
F32, BF16 = jnp.float32, jnp.bfloat16
SPAN, ROWS, COLS, TOK, RING, REPS = 64, 256, 512, 256, 8, 32
HALF = COLS // 2
LISTS = 8
decay, epsilon = 0.999, 1e-06
FIRST = 3
STREAMS = 5
STREAM_ROWS = 32 + 3 * SPAN


def split(x):
    hi = x.astype(BF16)
    return hi, (x - hi.astype(F32)).astype(BF16)


def constants():
    freq = np.arange(SPAN, dtype=np.float64)[:, None]
    sample = np.arange(SPAN, dtype=np.float64)[None, :]
    basis = np.cos(np.pi * (2.0 * sample + 1.0) * freq / (2.0 * SPAN))
    basis = basis * np.where(freq == 0, np.sqrt(1.0 / SPAN), np.sqrt(2.0 / SPAN))
    hi = basis.astype(BF16)
    lo = (basis - hi.astype(np.float64)).astype(BF16)

    def left(a, b):
        return np.concatenate([a, a, b, b], axis=1)

    def right(a):
        return np.kron(np.eye(4), a.astype(np.float64)).astype(BF16)

    lefts = np.stack([left(hi, lo), left(hi.T, lo.T)])
    rights = np.stack([right(hi.T), right(lo.T), right(hi), right(lo), right(np.ones((SPAN, SPAN)))])
    return lefts, rights


def dot(a, b):
    return jnp.dot(a, b, preferred_element_type=F32)


def dot_lanes(a, b):
    return lax.dot_general(a, b, (((1,), (1,)), ((), ())), preferred_element_type=F32)


def from_left(const, x):
    hi, lo = split(x)
    return dot(const, jnp.concatenate([hi, lo, hi, lo], axis=0))


def from_right(x, const_hi, const_lo):
    hi, lo = split(x)
    both = dot(jnp.concatenate([hi, lo], axis=0), const_hi)
    return both[: x.shape[0]] + both[x.shape[0] :] + dot(hi, const_lo)


def offset(way, stream, step):
    return (way * STREAMS + stream) * STREAM_ROWS + (0 if step == 0 else 32 + SPAN * (step - 1))


def kernel(
    x_hbm, g_hbm, m_hbm, sel_ref, left_ref, right_ref, new_hbm, upd_hbm,
    x_in, xt, x_got, g_own, g_got, mom, sums_out, sums_in, b_out, b_in, part, grad, coef, mask,
    ids, vals, l_hot, r_hot, r_own, new_v, upd_v,
    load_sem, xs_sem, xr_sem, zs_sem, zr_sem, is_sem, ir_sem, vs_sem, vr_sem, out_sem,
):
    rep, fsdp = lax.axis_index("rep"), lax.axis_index("fsdp")
    core, y, x_lo = rep % 2, (rep // 2) % 8, rep // 16
    z, x_hi = fsdp // 2, fsdp % 2
    partner = (rep, z * 2 + 1 - x_hi)
    ways = [(rep, ((z + 1) % RING) * 2 + x_hi), (rep, ((z + RING - 1) % RING) * 2 + x_hi)]
    peers = [
        (((x_lo + dx) % 2) * 16 + ((y + dy) % 8) * 2 + (core + dc) % 2, fsdp)
        for dy in (4, 3, 5, 2, 6, 1, 7, 0)
        for dx in (0, 1)
        for dc in (0, 1)
        if (dy, dx, dc) != (0, 0, 0)
    ]

    g_load = pltpu.make_async_copy(g_hbm.at[0], g_own, load_sem.at[0])
    g_load.start()
    order = (4, 3, 5, 2, 6, 1, 7, 0)
    x_loads = {}
    for n, dz in enumerate(order):
        for kind in (1, 0):
            column = ((z + dz) % RING) * 512 + (x_hi if kind == 0 else 1 - x_hi) * 256
            cp = pltpu.make_async_copy(
                x_hbm.at[0, :, pl.ds(pl.multiple_of(column, 256), 256)],
                x_in.at[dz, kind],
                load_sem.at[2 + 2 * n + kind],
            )
            cp.start()
            x_loads[dz, kind] = cp
    m_load = pltpu.make_async_copy(m_hbm.at[0], mom, load_sem.at[1])
    m_load.start()

    barrier = pltpu.get_barrier_semaphore()
    for device in [partner, *ways, *peers]:
        pl.semaphore_signal(barrier, inc=1, device_id=device, device_id_type=MESH)

    rows = []
    for a in range(4):
        for h in range(2):
            rows.append(jnp.concatenate([sel_ref[0, a, 4 * h + j : 4 * h + j + 1, :] for j in range(4)], axis=1))
    own_ids = jnp.concatenate(rows, axis=0)
    ids[pl.ds(rep, 1)] = own_ids[None]

    pl.semaphore_wait(barrier, 3 + len(peers))

    g_load.wait()

    def remote(src, dst, send_sem, recv_sem, device):
        cp = pltpu.make_async_remote_copy(
            src_ref=src, dst_ref=dst, send_sem=send_sem, recv_sem=recv_sem, device_id=device, device_id_type=MESH
        )
        cp.start()
        return cp

    x_sends = [remote(g_own, g_got, xs_sem.at[8], xr_sem.at[8], partner)]
    id_sends = [
        remote(ids.at[pl.ds(rep, 1)], ids.at[pl.ds(rep, 1)], is_sem.at[0], ir_sem.at[0], device) for device in peers
    ]
    for dz in order:
        for kind in (1, 0):
            x_loads[dz, kind].wait()
            xt[dz, kind] = x_in[dz, kind].T
        x_sends.append(
            remote(
                xt.at[dz, 1, pl.ds(0, FIRST * SPAN)], x_got.at[dz], xs_sem.at[dz], xr_sem.at[dz], partner
            )
        )

    def wait_x(dz):
        x_sends[1 + order.index(dz)].wait_recv()

    def product(stream, dz):
        if stream < FIRST:
            at = pl.ds(stream * SPAN, SPAN)
            return dot(xt[dz, 0, at], g_own[...]) + dot(x_got[dz, at], g_got[...])
        return dot(xt[dz, 0 if stream == 3 else 1, pl.ds(FIRST * SPAN, SPAN)], g_own[...])

    z_copies = {}

    def send_sum(way, stream, step):
        size = 32 if step == 0 else SPAN
        at = pl.ds(offset(way, stream, step), size)
        z_copies[way, stream, step] = remote(
            sums_out.at[at], sums_in.at[at], zs_sem.at[0], zr_sem.at[way, stream, step], ways[way]
        )

    def arrived(way, stream, step):
        z_copies[way, stream, step].wait_recv()
        size = 32 if step == 0 else SPAN
        return sums_in[pl.ds(offset(way, stream, step), size), :].astype(F32)

    def chain(stream, step):
        if step == 0:
            term = product(stream, 4).astype(BF16)
            for way in range(2):
                sums_out[pl.ds(offset(way, stream, 0), 32), :] = term[32 * way : 32 * way + 32]
                send_sum(way, stream, 0)
            return
        for way in range(2):
            term = product(stream, 4 - step if way == 0 else 4 + step)
            got = arrived(way, stream, step - 1)
            at = offset(way, stream, step)
            if step == 1:
                for part_ in range(2):
                    piece = term[32 * part_ : 32 * part_ + 32]
                    piece = piece + got if part_ == way else piece
                    sums_out[pl.ds(at + 32 * part_, 32), :] = piece.astype(BF16)
            else:
                sums_out[pl.ds(at, SPAN), :] = (term + got).astype(BF16)
            send_sum(way, stream, step)

    def finish(stream):
        return product(stream, 0) + arrived(0, stream, 3) + arrived(1, stream, 3)

    lane = lax.broadcasted_iota(jnp.int32, (1, 128), 1)
    count_u = lax.broadcasted_iota(jnp.int32, (SPAN, 128), 0)
    count_n = lax.broadcasted_iota(jnp.int32, (HALF, 128), 0)

    def hot(row):
        by_row = (row >> 6) == count_u
        by_column = (row & 63) + (lane >> 5) * SPAN == count_n
        return by_row.astype(F32).astype(BF16), by_column.astype(F32).astype(BF16)

    def build(first, count):
        def one(r, carry):
            at = pl.ds(pl.multiple_of(r * 128, 128), 128)
            for s in range(LISTS):
                l, n = hot(ids[r, s : s + 1, :])
                l_hot[s, :, at] = l
                r_hot[s, :, at] = n
            return carry

        lax.fori_loop(first, first + count, one, 0)

    def own_mask():
        for s in range(LISTS):
            l, n = hot(own_ids[s : s + 1])
            r_own[s] = n
            a, h = s // 2, s % 2
            mask[pl.ds(a * SPAN, SPAN), pl.ds(h * HALF, HALF)] = dot_lanes(l, n)

    def transform(a):
        at = pl.ds(a * SPAN, SPAN)
        stepped = decay * mom[at, :] + grad[at, :]
        grad[at, :] = stepped
        partly = from_left(left_ref[0], stepped)
        kept = []
        for h in range(2):
            c = from_right(partly[:, h * HALF : (h + 1) * HALF], right_ref[0], right_ref[1])
            coef[at, pl.ds(h * HALF, HALF)] = c
            s = 2 * a + h
            hi, lo = split(c)
            both = dot(jnp.concatenate([hi, lo], axis=0), r_own[s])
            by_row = (own_ids[s : s + 1] >> 6) == count_u
            kept.append(jnp.sum(jnp.where(by_row, both[:SPAN] + both[SPAN:], 0.0), axis=0, keepdims=True))
        vals[pl.ds(rep, 1), pl.ds(2 * a, 2)] = jnp.concatenate(kept, axis=0)[None]

    chain(3, 0)
    chain(4, 0)
    own_mask()
    chain(3, 1)
    chain(4, 1)
    chain(3, 2)
    chain(4, 2)
    x_sends[0].wait_recv()
    wait_x(4)
    for s in range(FIRST):
        chain(s, 0)
    chain(4, 3)
    chain(3, 3)
    most = pltpu.make_async_remote_copy(
        src_ref=ids.at[pl.ds(0, REPS - 1)], dst_ref=ids.at[pl.ds(0, REPS - 1)],
        send_sem=is_sem.at[0], recv_sem=ir_sem.at[0], device_id=partner, device_id_type=MESH,
    )
    most.wait_recv()
    build(0, 8)
    wait_x(3)
    wait_x(5)
    for s in range(FIRST):
        chain(s, 1)
    build(8, 8)
    wait_x(2)
    wait_x(6)
    for s in range(FIRST):
        chain(s, 2)
    b_out[...] = finish(4).astype(BF16)
    b_send = remote(b_out, b_in, xs_sem.at[9], xr_sem.at[9], partner)
    build(16, 8)
    wait_x(1)
    wait_x(7)
    for s in range(FIRST):
        chain(s, 3)
    build(24, 8)
    m_load.wait()
    own = finish(3)
    b_send.wait_recv()
    grad[pl.ds(FIRST * SPAN, SPAN), :] = own + b_in[...].astype(F32)
    transform(3)
    wait_x(0)
    for s in range(FIRST):
        grad[pl.ds(s * SPAN, SPAN), :] = finish(s)
        transform(s)

    val_sends = [
        remote(vals.at[pl.ds(rep, 1)], vals.at[pl.ds(rep, 1)], vs_sem.at[0], vr_sem.at[0], device) for device in peers
    ]
    for a in range(4):
        at = pl.ds(a * SPAN, SPAN)
        partly = from_left(left_ref[1], coef[at, :] * mask[at, :])
        for h in range(2):
            cols = pl.ds(h * HALF, HALF)
            own = from_right(partly[:, h * HALF : (h + 1) * HALF], right_ref[2], right_ref[3])
            new_v[at, cols] = grad[at, cols] - own
    new_store = pltpu.make_async_copy(new_v, new_hbm.at[0], out_sem.at[0])
    new_store.start()

    most_vals = pltpu.make_async_remote_copy(
        src_ref=vals.at[pl.ds(0, REPS - 1)], dst_ref=vals.at[pl.ds(0, REPS - 1)],
        send_sem=vs_sem.at[0], recv_sem=vr_sem.at[0], device_id=partner, device_id_type=MESH,
    )
    most_vals.wait_recv()
    total = []
    for s in range(LISTS):
        weighted = jnp.concatenate(
            [l_hot[s, :, r * 128 : (r + 1) * 128] * vals[r, s : s + 1, :].astype(BF16) for r in range(REPS)], axis=1
        )
        total.append(dot_lanes(weighted, r_hot[s]))
    power = jnp.concatenate([jnp.sum(t * t, axis=0, keepdims=True) for t in total], axis=0)
    hi, lo = split(power)
    power = dot(hi, right_ref[4]) + dot(lo, right_ref[4])
    scale = lax.rsqrt(power * (1.0 / (SPAN * SPAN)) + epsilon)
    for s in range(LISTS):
        decoded = from_right(from_left(left_ref[1], total[s]), right_ref[2], right_ref[3])
        at = (pl.ds((s // 2) * SPAN, SPAN), pl.ds((s % 2) * HALF, HALF))
        upd_v[at] = (decoded * scale[s : s + 1]).astype(BF16)
    upd_store = pltpu.make_async_copy(upd_v, upd_hbm, out_sem.at[1])
    upd_store.start()

    for cp in x_sends:
        cp.wait_send()
    b_send.wait_send()
    pltpu.make_async_remote_copy(
        src_ref=sums_out, dst_ref=sums_out, send_sem=zs_sem.at[0], recv_sem=zr_sem.at[0, 0, 0],
        device_id=partner, device_id_type=MESH,
    ).wait_send()
    most.wait_send()
    most_vals.wait_send()
    new_store.wait()
    upd_store.wait()


def local(inputs, up_grads, momentum, selected):
    lefts, rights = constants()
    vmem, hbm = pl.BlockSpec(memory_space=pltpu.VMEM), pl.BlockSpec(memory_space=pl.ANY)
    sums = STREAMS * 2 * STREAM_ROWS
    return pl.pallas_call(
        kernel,
        out_shape=(
            jax.ShapeDtypeStruct((1, ROWS, COLS), F32),
            jax.ShapeDtypeStruct((ROWS, COLS), BF16),
        ),
        in_specs=[hbm, hbm, hbm, vmem, vmem, vmem],
        out_specs=(hbm, hbm),
        scratch_shapes=[
            pltpu.VMEM((RING, 2, TOK, ROWS), BF16),
            pltpu.VMEM((RING, 2, ROWS, TOK), BF16),
            pltpu.VMEM((RING, FIRST * SPAN, TOK), BF16),
            pltpu.VMEM((TOK, COLS), BF16),
            pltpu.VMEM((TOK, COLS), BF16),
            pltpu.VMEM((ROWS, COLS), F32),
            pltpu.VMEM((sums, COLS), BF16),
            pltpu.VMEM((sums, COLS), BF16),
            pltpu.VMEM((SPAN, COLS), BF16),
            pltpu.VMEM((SPAN, COLS), BF16),
            pltpu.VMEM((SPAN, COLS), F32),
            pltpu.VMEM((ROWS, COLS), F32),
            pltpu.VMEM((ROWS, COLS), F32),
            pltpu.VMEM((ROWS, COLS), F32),
            pltpu.VMEM((REPS, LISTS, 128), jnp.int32),
            pltpu.VMEM((REPS, LISTS, 128), F32),
            pltpu.VMEM((LISTS, SPAN, REPS * 128), BF16),
            pltpu.VMEM((LISTS, HALF, REPS * 128), BF16),
            pltpu.VMEM((LISTS, HALF, 128), BF16),
            pltpu.VMEM((ROWS, COLS), F32),
            pltpu.VMEM((ROWS, COLS), BF16),
            pltpu.SemaphoreType.DMA((18,)),
            pltpu.SemaphoreType.DMA((10,)),
            pltpu.SemaphoreType.DMA((10,)),
            pltpu.SemaphoreType.DMA((1,)),
            pltpu.SemaphoreType.DMA((2, STREAMS, 4)),
            pltpu.SemaphoreType.DMA((1,)),
            pltpu.SemaphoreType.DMA((1,)),
            pltpu.SemaphoreType.DMA((1,)),
            pltpu.SemaphoreType.DMA((1,)),
            pltpu.SemaphoreType.DMA((2,)),
        ],
        compiler_params=pltpu.CompilerParams(
            collective_id=0, has_side_effects=True, vmem_limit_bytes=56 * 1024 * 1024
        ),
        cost_estimate=pl.CostEstimate(flops=4 * 10**9, bytes_accessed=8 * 10**6, transcendentals=0),
    )(inputs, up_grads, momentum, selected, jnp.asarray(lefts), jnp.asarray(rights))


def solution(mesh):
    placed = (
        P("rep", "fsdp", None),
        P("rep", "fsdp", None),
        P("rep", "fsdp", None),
        P("rep", "fsdp", None, None),
    )
    return jax.shard_map(
        local,
        mesh=mesh,
        in_specs=placed,
        out_specs=(P("rep", "fsdp", None), P("fsdp", None)),
        check_vma=False,
    )
```

```python
import jax
import jax.numpy as jnp
import numpy as np
from jax import lax
from jax.experimental import pallas as pl
from jax.experimental.pallas import tpu as pltpu
from jax.sharding import PartitionSpec as P

MESH = pl.DeviceIdType.MESH
F32, BF16 = jnp.float32, jnp.bfloat16
SPAN, ROWS, COLS, TOK, RING, REPS = 64, 256, 512, 256, 8, 32
HALF = COLS // 2
AROUND = (0, 4, 3, 5, 2, 6, 1, 7)
LISTS = 8
decay, epsilon = 0.999, 1e-06
FIRST = 3
STREAMS = 5
STREAM_ROWS = 32 + 3 * SPAN


def split(x):
    hi = x.astype(BF16)
    return hi, (x - hi.astype(F32)).astype(BF16)


def constants():
    freq = np.arange(SPAN, dtype=np.float64)[:, None]
    sample = np.arange(SPAN, dtype=np.float64)[None, :]
    basis = np.cos(np.pi * (2.0 * sample + 1.0) * freq / (2.0 * SPAN))
    basis = basis * np.where(freq == 0, np.sqrt(1.0 / SPAN), np.sqrt(2.0 / SPAN))
    hi = basis.astype(BF16)
    lo = (basis - hi.astype(np.float64)).astype(BF16)

    def left(a, b):
        return np.concatenate([a, a, b, b], axis=1)

    def right(a):
        return np.kron(np.eye(4), a.astype(np.float64)).astype(BF16)

    lefts = np.stack([left(hi, lo), left(hi.T, lo.T)])
    rights = np.stack([right(hi.T), right(lo.T), right(hi), right(lo), right(np.ones((SPAN, SPAN)))])
    return lefts, rights


def dot(a, b):
    return jnp.dot(a, b, preferred_element_type=F32)


def dot_lanes(a, b):
    return lax.dot_general(a, b, (((1,), (1,)), ((), ())), preferred_element_type=F32)


def from_left(const, x):
    hi, lo = split(x)
    return dot(const, jnp.concatenate([hi, lo, hi, lo], axis=0))


def from_right(x, const_hi, const_lo):
    hi, lo = split(x)
    both = dot(jnp.concatenate([hi, lo], axis=0), const_hi)
    return both[: x.shape[0]] + both[x.shape[0] :] + dot(hi, const_lo)


def offset(way, stream, step):
    return (way * STREAMS + stream) * STREAM_ROWS + (0 if step == 0 else 32 + SPAN * (step - 1))


def kernel(
    x_hbm, g_hbm, m_hbm, sel_hbm, left_hbm, right_hbm, new_hbm, upd_hbm,
    sel_ref, left_ref, right_ref, x_in, xt, x_got, g_own, g_got, mom, sums_out, sums_in, b_out, b_in, grad, coef, mask,
    ids, vals, l_hot, r_hot, r_own, total, new_v, upd_v,
    load_sem, xs_sem, xr_sem, zs_sem, zr_sem, is_sem, ir_sem, vs_sem, vr_sem, out_sem,
):
    rep, fsdp = lax.axis_index("rep"), lax.axis_index("fsdp")
    core, y, x_lo = rep % 2, (rep // 2) % 8, rep // 16
    z, x_hi = fsdp // 2, fsdp % 2
    partner = (rep, z * 2 + 1 - x_hi)
    ways = [(rep, ((z + 1) % RING) * 2 + x_hi), (rep, ((z + RING - 1) % RING) * 2 + x_hi)]
    near = [
        (((x_lo + dx) % 2) * 16 + y * 2 + (core + dc) % 2, fsdp) for dx in (0, 1) for dc in (0, 1) if dx + dc > 0
    ]
    far = {dy: (x_lo * 16 + ((y + dy) % 8) * 2 + core, fsdp) for dy in AROUND[1:]}

    barrier = pltpu.get_barrier_semaphore()
    for device in [partner, *ways, *near, *far.values()]:
        pl.semaphore_signal(barrier, inc=1, device_id=device, device_id_type=MESH)

    sel_load = pltpu.make_async_copy(sel_hbm, sel_ref, load_sem.at[18])
    sel_load.start()
    g_load = pltpu.make_async_copy(g_hbm.at[0], g_own, load_sem.at[0])
    g_load.start()
    order = (4, 3, 5, 2, 6, 1, 7, 0)
    x_loads = {}
    for n, dz in enumerate(order):
        for kind in (1, 0):
            column = ((z + dz) % RING) * 512 + (x_hi if kind == 0 else 1 - x_hi) * 256
            cp = pltpu.make_async_copy(
                x_hbm.at[0, :, pl.ds(pl.multiple_of(column, 256), 256)],
                x_in.at[dz, kind],
                load_sem.at[2 + 2 * n + kind],
            )
            cp.start()
            x_loads[dz, kind] = cp
    m_load = pltpu.make_async_copy(m_hbm.at[0], mom, load_sem.at[1])
    m_load.start()
    left_load = pltpu.make_async_copy(left_hbm, left_ref, load_sem.at[19])
    left_load.start()
    right_load = pltpu.make_async_copy(right_hbm, right_ref, load_sem.at[20])
    right_load.start()

    sel_load.wait()
    rows = []
    for a in range(4):
        for h in range(2):
            rows.append(jnp.concatenate([sel_ref[0, a, 4 * h + j : 4 * h + j + 1, :] for j in range(4)], axis=1))
    own_ids = jnp.concatenate(rows, axis=0)
    ids[0] = own_ids

    pl.semaphore_wait(barrier, 3 + len(near) + len(far))

    def remote(src, dst, send_sem, recv_sem, device):
        cp = pltpu.make_async_remote_copy(
            src_ref=src, dst_ref=dst, send_sem=send_sem, recv_sem=recv_sem, device_id=device, device_id_type=MESH
        )
        cp.start()
        return cp

    x_sends = {}

    def turn(*distances):
        for dz in distances:
            for kind in (1, 0):
                x_loads[dz, kind].wait()
                xt[dz, kind] = x_in[dz, kind].T
                if kind == 1:
                    x_sends[dz] = remote(
                        xt.at[dz, 1, pl.ds(0, FIRST * SPAN)], x_got.at[dz], xs_sem.at[dz], xr_sem.at[dz], partner
                    )

    def wait_x(dz):
        x_sends[dz].wait_recv()

    def product(stream, dz):
        if stream < FIRST:
            at = pl.ds(stream * SPAN, SPAN)
            return dot(xt[dz, 0, at], g_own[...]) + dot(x_got[dz, at], g_got[...])
        return dot(xt[dz, 0 if stream == 3 else 1, pl.ds(FIRST * SPAN, SPAN)], g_own[...])

    z_copies = {}

    def send_sum(way, stream, step):
        size = 32 if step == 0 else SPAN
        at = pl.ds(offset(way, stream, step), size)
        z_copies[way, stream, step] = remote(
            sums_out.at[at], sums_in.at[at], zs_sem.at[0], zr_sem.at[way, stream, step], ways[way]
        )

    def arrived(way, stream, step):
        z_copies[way, stream, step].wait_recv()
        size = 32 if step == 0 else SPAN
        return sums_in[pl.ds(offset(way, stream, step), size), :].astype(F32)

    def chain(stream, step):
        if step == 0:
            term = product(stream, 4).astype(BF16)
            for way in range(2):
                sums_out[pl.ds(offset(way, stream, 0), 32), :] = term[32 * way : 32 * way + 32]
                send_sum(way, stream, 0)
            return
        for way in range(2):
            term = product(stream, 4 - step if way == 0 else 4 + step)
            got = arrived(way, stream, step - 1)
            at = offset(way, stream, step)
            if step == 1:
                for part_ in range(2):
                    piece = term[32 * part_ : 32 * part_ + 32]
                    piece = piece + got if part_ == way else piece
                    sums_out[pl.ds(at + 32 * part_, 32), :] = piece.astype(BF16)
            else:
                sums_out[pl.ds(at, SPAN), :] = (term + got).astype(BF16)
            send_sum(way, stream, step)

    def finish(stream):
        return product(stream, 0) + arrived(0, stream, 3) + arrived(1, stream, 3)

    lane = lax.broadcasted_iota(jnp.int32, (1, 128), 1)
    count_u = lax.broadcasted_iota(jnp.int32, (SPAN, 128), 0)
    count_n = lax.broadcasted_iota(jnp.int32, (HALF, 128), 0)

    def hot(row):
        by_row = (row >> 6) == count_u
        by_column = (row & 63) + (lane >> 5) * SPAN == count_n
        return by_row.astype(F32).astype(BF16), by_column.astype(F32).astype(BF16)

    def send_near(slots, send_sem, recv_sem):
        for n, device in enumerate(near):
            remote(slots.at[0], slots.at[1 + n], send_sem.at[0], recv_sem.at[0], device)

    def send_far(slots, send_sem, recv_sem):
        landed(slots, recv_sem, 0)
        for dy, device in far.items():
            n = AROUND.index(8 - dy)
            remote(slots.at[pl.ds(0, 4)], slots.at[pl.ds(4 * n, 4)], send_sem.at[1], recv_sem.at[n], device)

    def of_size(slots, count, send_sem, recv_sem):
        at = slots.at[pl.ds(0, count)]
        return pltpu.make_async_remote_copy(
            src_ref=at, dst_ref=at, send_sem=send_sem, recv_sem=recv_sem, device_id=partner, device_id_type=MESH
        )

    def landed(slots, recv_sem, n):
        of_size(slots, 3 if n == 0 else 4, is_sem.at[0], recv_sem.at[n]).wait_recv()

    def sent(slots, send_sem):
        of_size(slots, 3, send_sem.at[0], ir_sem.at[0]).wait_send()
        of_size(slots, 28, send_sem.at[1], ir_sem.at[0]).wait_send()

    def build(first, count):
        def one(r, carry):
            at = pl.ds(pl.multiple_of(r * 128, 128), 128)
            for s in range(LISTS):
                l, n = hot(ids[r, s : s + 1, :])
                l_hot[s, :, at] = l
                r_hot[s, at, :] = n.T
            return carry

        lax.fori_loop(first, first + count, one, 0)

    def own_mask():
        for s in range(LISTS):
            l, n = hot(own_ids[s : s + 1])
            r_own[s] = n
            a, h = s // 2, s % 2
            mask[pl.ds(a * SPAN, SPAN), pl.ds(h * HALF, HALF)] = dot_lanes(l, n)

    def transform(a):
        at = pl.ds(a * SPAN, SPAN)
        stepped = decay * mom[at, :] + grad[at, :]
        grad[at, :] = stepped
        partly = from_left(left_ref[0], stepped)
        kept = []
        for h in range(2):
            c = from_right(partly[:, h * HALF : (h + 1) * HALF], right_ref[0], right_ref[1])
            coef[at, pl.ds(h * HALF, HALF)] = c
            s = 2 * a + h
            hi, lo = split(c)
            both = dot(jnp.concatenate([hi, lo], axis=0), r_own[s])
            by_row = (own_ids[s : s + 1] >> 6) == count_u
            kept.append(jnp.sum(jnp.where(by_row, both[:SPAN] + both[SPAN:], 0.0), axis=0, keepdims=True))
        vals[0, pl.ds(2 * a, 2)] = jnp.concatenate(kept, axis=0)

    send_near(ids, is_sem, ir_sem)
    g_send = remote(g_hbm.at[0], g_got, xs_sem.at[8], xr_sem.at[8], partner)
    turn(4)
    g_load.wait()
    chain(3, 0)
    chain(4, 0)
    turn(3, 5)
    send_far(ids, is_sem, ir_sem)
    chain(3, 1)
    chain(4, 1)
    turn(2, 6)
    chain(3, 2)
    chain(4, 2)
    turn(1, 7)
    g_send.wait_recv()
    wait_x(4)
    for s in range(FIRST):
        chain(s, 0)
    chain(4, 3)
    chain(3, 3)
    turn(0)
    own_mask()
    build(0, 4)
    wait_x(3)
    wait_x(5)
    chain(0, 1)
    for n in range(1, 8):
        landed(ids, ir_sem, n)
    build(4, 3)
    chain(1, 1)
    build(7, 3)
    chain(2, 1)
    build(10, 2)
    wait_x(2)
    wait_x(6)
    for s in range(FIRST):
        chain(s, 2)
        build(12 + 3 * s, 3)
    b_out[...] = finish(4).astype(BF16)
    b_send = remote(b_out, b_in, xs_sem.at[9], xr_sem.at[9], partner)
    wait_x(1)
    wait_x(7)
    for s in range(FIRST):
        chain(s, 3)
        build(21 + 3 * s, 3)
    build(30, 2)
    m_load.wait()
    left_load.wait()
    right_load.wait()
    own = finish(3)
    b_send.wait_recv()
    grad[pl.ds(FIRST * SPAN, SPAN), :] = own + b_in[...].astype(F32)
    transform(3)
    wait_x(0)
    for s in range(FIRST):
        grad[pl.ds(s * SPAN, SPAN), :] = finish(s)
        transform(s)

    send_near(vals, vs_sem, vr_sem)
    for a in range(4):
        if a == 2:
            send_far(vals, vs_sem, vr_sem)
        at = pl.ds(a * SPAN, SPAN)
        partly = from_left(left_ref[1], coef[at, :] * mask[at, :])
        for h in range(2):
            cols = pl.ds(h * HALF, HALF)
            own = from_right(partly[:, h * HALF : (h + 1) * HALF], right_ref[2], right_ref[3])
            new_v[at, cols] = grad[at, cols] - own
    new_store = pltpu.make_async_copy(new_v, new_hbm.at[0], out_sem.at[0])
    new_store.start()

    for first, last in ((0, 1), (1, 4), (4, 6), (6, 8)):
        for n in range(max(first, 1), last):
            landed(vals, vr_sem, n)
        for s in range(LISTS):
            weighted = jnp.concatenate(
                [
                    l_hot[s, :, r * 128 : (r + 1) * 128] * vals[r, s : s + 1, :].astype(BF16)
                    for r in range(4 * first, 4 * last)
                ],
                axis=1,
            )
            term = dot(weighted, r_hot[s, pl.ds(4 * first * 128, 4 * (last - first) * 128)])
            total[s] = term if first == 0 else total[s] + term
    power = jnp.concatenate([jnp.sum(total[s] * total[s], axis=0, keepdims=True) for s in range(LISTS)], axis=0)
    hi, lo = split(power)
    power = dot(hi, right_ref[4]) + dot(lo, right_ref[4])
    scale = lax.rsqrt(power * (1.0 / (SPAN * SPAN)) + epsilon)
    for s in range(LISTS):
        decoded = from_right(from_left(left_ref[1], total[s]), right_ref[2], right_ref[3])
        at = (pl.ds((s // 2) * SPAN, SPAN), pl.ds((s % 2) * HALF, HALF))
        upd_v[at] = (decoded * scale[s : s + 1]).astype(BF16)
    upd_store = pltpu.make_async_copy(upd_v, upd_hbm, out_sem.at[1])
    upd_store.start()

    g_send.wait_send()
    for cp in x_sends.values():
        cp.wait_send()
    b_send.wait_send()
    pltpu.make_async_remote_copy(
        src_ref=sums_out, dst_ref=sums_out, send_sem=zs_sem.at[0], recv_sem=zr_sem.at[0, 0, 0],
        device_id=partner, device_id_type=MESH,
    ).wait_send()
    sent(ids, is_sem)
    sent(vals, vs_sem)
    new_store.wait()
    upd_store.wait()


def hand_on(new_ref, upd_ref, new_out, upd_out, new_v, upd_v, load_sem, store_sem):
    loads, stores = [], []
    for n in range(8):
        held, src, dst = (new_v, new_ref.at[0], new_out.at[0]) if n < 4 else (upd_v, upd_ref, upd_out)
        at = pl.ds((n % 4) * SPAN, SPAN)
        loads.append(pltpu.make_async_copy(src.at[at], held.at[at], load_sem.at[n]))
        stores.append(pltpu.make_async_copy(held.at[at], dst.at[at], store_sem.at[n]))
        loads[n].start()
    for load, store in zip(loads, stores):
        load.wait()
        store.start()
    for store in stores:
        store.wait()


def local(inputs, up_grads, momentum, selected):
    lefts, rights = constants()
    hbm = pl.BlockSpec(memory_space=pl.ANY)
    sums = STREAMS * 2 * STREAM_ROWS
    new, upd = pl.pallas_call(
        kernel,
        out_shape=(
            jax.ShapeDtypeStruct((1, ROWS, COLS), F32),
            jax.ShapeDtypeStruct((ROWS, COLS), BF16),
        ),
        in_specs=[hbm] * 6,
        out_specs=(hbm, hbm),
        scratch_shapes=[
            pltpu.VMEM((1, 4, 8, 32), jnp.int32),
            pltpu.VMEM(lefts.shape, BF16),
            pltpu.VMEM(rights.shape, BF16),
            pltpu.VMEM((RING, 2, TOK, ROWS), BF16),
            pltpu.VMEM((RING, 2, ROWS, TOK), BF16),
            pltpu.VMEM((RING, FIRST * SPAN, TOK), BF16),
            pltpu.VMEM((TOK, COLS), BF16),
            pltpu.VMEM((TOK, COLS), BF16),
            pltpu.VMEM((ROWS, COLS), F32),
            pltpu.VMEM((sums, COLS), BF16),
            pltpu.VMEM((sums, COLS), BF16),
            pltpu.VMEM((SPAN, COLS), BF16),
            pltpu.VMEM((SPAN, COLS), BF16),
                pltpu.VMEM((ROWS, COLS), F32),
            pltpu.VMEM((ROWS, COLS), F32),
            pltpu.VMEM((ROWS, COLS), F32),
            pltpu.VMEM((REPS, LISTS, 128), jnp.int32),
            pltpu.VMEM((REPS, LISTS, 128), F32),
            pltpu.VMEM((LISTS, SPAN, REPS * 128), BF16),
            pltpu.VMEM((LISTS, REPS * 128, HALF), BF16),
            pltpu.VMEM((LISTS, HALF, 128), BF16),
            pltpu.VMEM((LISTS, SPAN, HALF), F32),
            pltpu.VMEM((ROWS, COLS), F32),
            pltpu.VMEM((ROWS, COLS), BF16),
            pltpu.SemaphoreType.DMA((21,)),
            pltpu.SemaphoreType.DMA((10,)),
            pltpu.SemaphoreType.DMA((10,)),
            pltpu.SemaphoreType.DMA((1,)),
            pltpu.SemaphoreType.DMA((2, STREAMS, 4)),
            pltpu.SemaphoreType.DMA((2,)),
            pltpu.SemaphoreType.DMA((len(AROUND),)),
            pltpu.SemaphoreType.DMA((2,)),
            pltpu.SemaphoreType.DMA((len(AROUND),)),
            pltpu.SemaphoreType.DMA((2,)),
        ],
        compiler_params=pltpu.CompilerParams(
            collective_id=0, has_side_effects=True, vmem_limit_bytes=56 * 1024 * 1024
        ),
        cost_estimate=pl.CostEstimate(flops=4 * 10**9, bytes_accessed=8 * 10**6, transcendentals=0),
    )(inputs, up_grads, momentum, selected, jnp.asarray(lefts), jnp.asarray(rights))
    return pl.pallas_call(
        hand_on,
        out_shape=(jax.ShapeDtypeStruct((1, ROWS, COLS), F32), jax.ShapeDtypeStruct((ROWS, COLS), BF16)),
        in_specs=[hbm, hbm],
        out_specs=(hbm, hbm),
        scratch_shapes=[
            pltpu.VMEM((ROWS, COLS), F32),
            pltpu.VMEM((ROWS, COLS), BF16),
            pltpu.SemaphoreType.DMA((8,)),
            pltpu.SemaphoreType.DMA((8,)),
        ],
    )(new, upd)


def solution(mesh):
    placed = (
        P("rep", "fsdp", None),
        P("rep", "fsdp", None),
        P("rep", "fsdp", None),
        P("rep", "fsdp", None, None),
    )
    return jax.shard_map(
        local,
        mesh=mesh,
        in_specs=placed,
        out_specs=(P("rep", "fsdp", None), P("fsdp", None)),
        check_vma=False,
    )
```

```python
import jax
import jax.numpy as jnp
import numpy as np
from jax import lax
from jax.experimental import pallas as pl
from jax.experimental.pallas import tpu as pltpu
from jax.sharding import PartitionSpec as P

MESH = pl.DeviceIdType.MESH
F32, BF16 = jnp.float32, jnp.bfloat16
SPAN, ROWS, COLS, TOK, RING, REPS = 64, 256, 512, 256, 8, 32
HALF = COLS // 2
AROUND = (0, 4, 3, 5, 2, 6, 1, 7)
GROUP = 8
LISTS = 8
decay, epsilon = 0.999, 1e-06
FIRST = 3
STREAMS = 5
STREAM_ROWS = 32 + 3 * SPAN


def split(x):
    hi = x.astype(BF16)
    return hi, (x - hi.astype(F32)).astype(BF16)


def constants():
    freq = np.arange(SPAN, dtype=np.float64)[:, None]
    sample = np.arange(SPAN, dtype=np.float64)[None, :]
    basis = np.cos(np.pi * (2.0 * sample + 1.0) * freq / (2.0 * SPAN))
    basis = basis * np.where(freq == 0, np.sqrt(1.0 / SPAN), np.sqrt(2.0 / SPAN))
    hi = basis.astype(BF16)
    lo = (basis - hi.astype(np.float64)).astype(BF16)

    def left(a, b):
        return np.concatenate([a, a, b, b], axis=1)

    def right(a):
        return np.kron(np.eye(4), a.astype(np.float64)).astype(BF16)

    lefts = np.stack([left(hi, lo), left(hi.T, lo.T)])
    rights = np.stack([right(hi.T), right(lo.T), right(hi), right(lo), right(np.ones((SPAN, SPAN)))])
    return lefts, rights


def dot(a, b):
    return jnp.dot(a, b, preferred_element_type=F32)


def dot_lanes(a, b):
    return lax.dot_general(a, b, (((1,), (1,)), ((), ())), preferred_element_type=F32)


def from_left(const, x):
    hi, lo = split(x)
    return dot(const, jnp.concatenate([hi, lo, hi, lo], axis=0))


def from_right(x, const_hi, const_lo):
    hi, lo = split(x)
    both = dot(jnp.concatenate([hi, lo], axis=0), const_hi)
    return both[: x.shape[0]] + both[x.shape[0] :] + dot(hi, const_lo)


def offset(way, stream, step):
    return (way * STREAMS + stream) * STREAM_ROWS + (0 if step == 0 else 32 + SPAN * (step - 1))


def kernel(
    x_hbm, g_hbm, m_hbm, sel_hbm, left_hbm, right_hbm, new_hbm, upd_hbm,
    sel_ref, left_ref, right_ref, x_in, xt, x_got, g_own, g_got, mom, sums_out, sums_in, b_out, b_in, grad, coef, mask,
    ids, vals, l_hot, r_hot, r_own, total, new_v, upd_v,
    load_sem, xs_sem, xr_sem, zs_sem, zr_sem, is_sem, ir_sem, vs_sem, vr_sem, out_sem,
):
    rep, fsdp = lax.axis_index("rep"), lax.axis_index("fsdp")
    core, y, x_lo = rep % 2, (rep // 2) % 8, rep // 16
    z, x_hi = fsdp // 2, fsdp % 2
    partner = (rep, z * 2 + 1 - x_hi)
    ways = [(rep, ((z + 1) % RING) * 2 + x_hi), (rep, ((z + RING - 1) % RING) * 2 + x_hi)]
    def there(dy, dx, dc):
        return (((x_lo + dx) % 2) * 16 + ((y + dy) % 8) * 2 + (core + dc) % 2, fsdp)

    around = [(dy, dx, dc) for dy in AROUND for dx in (0, 1) for dc in (0, 1)]
    near = [there(*d) for d in around[1:4]]
    far = {dy: there(dy, 0, 0) for dy in AROUND[1:]}

    order = (4, 3, 5, 2, 6, 1, 7, 0)
    x_loads = {}

    def load_x(dz, kind):
        column = ((z + dz) % RING) * 512 + (x_hi if kind == 0 else 1 - x_hi) * 256
        x_loads[dz, kind] = pltpu.make_async_copy(
            x_hbm.at[0, :, pl.ds(pl.multiple_of(column, 256), 256)], x_in.at[dz, kind], load_sem.at[2 * dz + kind]
        )
        x_loads[dz, kind].start()

    sel_load = pltpu.make_async_copy(sel_hbm, sel_ref, load_sem.at[16])
    g_load = pltpu.make_async_copy(g_hbm.at[0], g_own, load_sem.at[17])
    sel_load.start()
    load_x(4, 1)
    load_x(4, 0)
    g_load.start()

    barrier = pltpu.get_barrier_semaphore()
    for device in [partner, *ways, *(there(*d) for d in around[1:])]:
        pl.semaphore_signal(barrier, inc=1, device_id=device, device_id_type=MESH)

    for dz in order[1:]:
        load_x(dz, 1)
        load_x(dz, 0)
    m_load = pltpu.make_async_copy(m_hbm.at[0], mom, load_sem.at[18])
    left_load = pltpu.make_async_copy(left_hbm, left_ref, load_sem.at[19])
    right_load = pltpu.make_async_copy(right_hbm, right_ref, load_sem.at[20])
    for cp in (m_load, left_load, right_load):
        cp.start()

    sel_load.wait()
    rows = []
    for a in range(4):
        for h in range(2):
            rows.append(jnp.concatenate([sel_ref[0, a, 4 * h + j : 4 * h + j + 1, :] for j in range(4)], axis=1))
    own_ids = jnp.concatenate(rows, axis=0)
    ids[0] = own_ids

    pl.semaphore_wait(barrier, 3 + REPS - 1)

    def remote(src, dst, send_sem, recv_sem, device):
        cp = pltpu.make_async_remote_copy(
            src_ref=src, dst_ref=dst, send_sem=send_sem, recv_sem=recv_sem, device_id=device, device_id_type=MESH
        )
        cp.start()
        return cp

    x_sends = {}

    def turn(*distances):
        for dz in distances:
            for kind in (1, 0):
                x_loads[dz, kind].wait()
                xt[dz, kind] = x_in[dz, kind].T
                if kind == 1:
                    x_sends[dz] = remote(
                        xt.at[dz, 1, pl.ds(0, FIRST * SPAN)], x_got.at[dz], xs_sem.at[dz], xr_sem.at[dz], partner
                    )

    def wait_x(dz):
        x_sends[dz].wait_recv()

    def product(stream, dz):
        if stream < FIRST:
            at = pl.ds(stream * SPAN, SPAN)
            return dot(xt[dz, 0, at], g_own[...]) + dot(x_got[dz, at], g_got[...])
        return dot(xt[dz, 0 if stream == 3 else 1, pl.ds(FIRST * SPAN, SPAN)], g_own[...])

    z_copies = {}

    def send_sum(way, stream, step):
        size = 32 if step == 0 else SPAN
        at = pl.ds(offset(way, stream, step), size)
        z_copies[way, stream, step] = remote(
            sums_out.at[at], sums_in.at[at], zs_sem.at[0], zr_sem.at[way, stream, step], ways[way]
        )

    def arrived(way, stream, step):
        z_copies[way, stream, step].wait_recv()
        size = 32 if step == 0 else SPAN
        return sums_in[pl.ds(offset(way, stream, step), size), :].astype(F32)

    def chain(stream, step):
        if step == 0:
            term = product(stream, 4).astype(BF16)
            for way in range(2):
                sums_out[pl.ds(offset(way, stream, 0), 32), :] = term[32 * way : 32 * way + 32]
                send_sum(way, stream, 0)
            return
        for way in range(2):
            term = product(stream, 4 - step if way == 0 else 4 + step)
            got = arrived(way, stream, step - 1)
            at = offset(way, stream, step)
            if step == 1:
                for part_ in range(2):
                    piece = term[32 * part_ : 32 * part_ + 32]
                    piece = piece + got if part_ == way else piece
                    sums_out[pl.ds(at + 32 * part_, 32), :] = piece.astype(BF16)
            else:
                sums_out[pl.ds(at, SPAN), :] = (term + got).astype(BF16)
            send_sum(way, stream, step)

    def finish(stream):
        return product(stream, 0) + arrived(0, stream, 3) + arrived(1, stream, 3)

    lane = lax.broadcasted_iota(jnp.int32, (1, 128), 1)
    count_u = lax.broadcasted_iota(jnp.int32, (SPAN, 128), 0)
    count_n = lax.broadcasted_iota(jnp.int32, (HALF, 128), 0)

    def hot(row):
        by_row = (row >> 6) == count_u
        by_column = (row & 63) + (lane >> 5) * SPAN == count_n
        return by_row.astype(F32).astype(BF16), by_column.astype(F32).astype(BF16)

    def send_near():
        for n, device in enumerate(near):
            remote(ids.at[0], ids.at[1 + n], is_sem.at[0], ir_sem.at[0], device)

    def send_far():
        landed(0)
        for dy, device in far.items():
            n = AROUND.index(8 - dy)
            remote(ids.at[pl.ds(0, 4)], ids.at[pl.ds(4 * n, 4)], is_sem.at[1], ir_sem.at[n], device)

    def of_size(slots, count, send_sem, recv_sem):
        at = slots.at[pl.ds(0, count)]
        return pltpu.make_async_remote_copy(
            src_ref=at, dst_ref=at, send_sem=send_sem, recv_sem=recv_sem, device_id=partner, device_id_type=MESH
        )

    def landed(n):
        of_size(ids, 3 if n == 0 else 4, is_sem.at[0], ir_sem.at[n]).wait_recv()

    def build(first, count):
        def one(r, carry):
            at = pl.ds(pl.multiple_of(r * 128, 128), 128)
            for s in range(LISTS):
                l, n = hot(ids[r, s : s + 1, :])
                l_hot[s, :, at] = l
                r_hot[s, at, :] = n.T
            return carry

        lax.fori_loop(first, first + count, one, 0)

    def own_mask():
        for s in range(LISTS):
            l, n = hot(own_ids[s : s + 1])
            r_own[s] = n
            a, h = s // 2, s % 2
            mask[pl.ds(a * SPAN, SPAN), pl.ds(h * HALF, HALF)] = dot_lanes(l, n)

    def transform(a):
        at = pl.ds(a * SPAN, SPAN)
        stepped = decay * mom[at, :] + grad[at, :]
        grad[at, :] = stepped
        partly = from_left(left_ref[0], stepped)
        kept = []
        for h in range(2):
            c = from_right(partly[:, h * HALF : (h + 1) * HALF], right_ref[0], right_ref[1])
            coef[at, pl.ds(h * HALF, HALF)] = c
            s = 2 * a + h
            hi, lo = split(c)
            both = dot(jnp.concatenate([hi, lo], axis=0), r_own[s])
            by_row = (own_ids[s : s + 1] >> 6) == count_u
            kept.append(jnp.sum(jnp.where(by_row, both[:SPAN] + both[SPAN:], 0.0), axis=0, keepdims=True))
        vals[0, pl.ds(2 * a, 2)] = jnp.concatenate(kept, axis=0)

    send_near()
    g_send = remote(g_hbm.at[0], g_got, xs_sem.at[8], xr_sem.at[8], partner)
    turn(4)
    g_load.wait()
    chain(3, 0)
    chain(4, 0)
    turn(3, 5)
    send_far()
    chain(3, 1)
    chain(4, 1)
    turn(2, 6)
    chain(3, 2)
    chain(4, 2)
    turn(1, 7)
    g_send.wait_recv()
    wait_x(4)
    for s in range(FIRST):
        chain(s, 0)
    chain(4, 3)
    chain(3, 3)
    turn(0)
    own_mask()
    build(0, 4)
    wait_x(3)
    wait_x(5)
    chain(0, 1)
    for n in range(1, 8):
        landed(n)
    build(4, 3)
    chain(1, 1)
    build(7, 3)
    chain(2, 1)
    build(10, 2)
    wait_x(2)
    wait_x(6)
    for s in range(FIRST):
        chain(s, 2)
        build(12 + 3 * s, 3)
    b_out[...] = finish(4).astype(BF16)
    b_send = remote(b_out, b_in, xs_sem.at[9], xr_sem.at[9], partner)
    wait_x(1)
    wait_x(7)
    for s in range(FIRST):
        chain(s, 3)
        build(21 + 3 * s, 3)
    build(30, 2)
    m_load.wait()
    left_load.wait()
    right_load.wait()
    own = finish(3)
    b_send.wait_recv()
    grad[pl.ds(FIRST * SPAN, SPAN), :] = own + b_in[...].astype(F32)
    transform(3)
    wait_x(0)
    for s in range(FIRST):
        grad[pl.ds(s * SPAN, SPAN), :] = finish(s)
        transform(s)

    for dy, dx, dc in around[1:]:
        slot = around.index(((8 - dy) % 8, dx, dc))
        remote(vals.at[0], vals.at[slot], vs_sem.at[0], vr_sem.at[slot // GROUP], there(dy, dx, dc))
    for a in range(4):
        at = pl.ds(a * SPAN, SPAN)
        partly = from_left(left_ref[1], coef[at, :] * mask[at, :])
        for h in range(2):
            cols = pl.ds(h * HALF, HALF)
            own = from_right(partly[:, h * HALF : (h + 1) * HALF], right_ref[2], right_ref[3])
            new_v[at, cols] = grad[at, cols] - own
    new_store = pltpu.make_async_copy(new_v, new_hbm.at[0], out_sem.at[0])
    new_store.start()

    for group in range(REPS // GROUP):
        of_size(vals, GROUP - (group == 0), vs_sem.at[0], vr_sem.at[group]).wait_recv()
        first, last = group * GROUP, (group + 1) * GROUP
        for s in range(LISTS):
            weighted = jnp.concatenate(
                [l_hot[s, :, r * 128 : (r + 1) * 128] * vals[r, s : s + 1, :].astype(BF16) for r in range(first, last)],
                axis=1,
            )
            term = dot(weighted, r_hot[s, pl.ds(first * 128, GROUP * 128)])
            total[s] = term if group == 0 else total[s] + term
    power = jnp.concatenate([jnp.sum(total[s] * total[s], axis=0, keepdims=True) for s in range(LISTS)], axis=0)
    hi, lo = split(power)
    power = dot(hi, right_ref[4]) + dot(lo, right_ref[4])
    scale = lax.rsqrt(power * (1.0 / (SPAN * SPAN)) + epsilon)
    for s in range(LISTS):
        decoded = from_right(from_left(left_ref[1], total[s]), right_ref[2], right_ref[3])
        at = (pl.ds((s // 2) * SPAN, SPAN), pl.ds((s % 2) * HALF, HALF))
        upd_v[at] = (decoded * scale[s : s + 1]).astype(BF16)
    upd_store = pltpu.make_async_copy(upd_v, upd_hbm, out_sem.at[1])
    upd_store.start()

    g_send.wait_send()
    for cp in x_sends.values():
        cp.wait_send()
    b_send.wait_send()
    pltpu.make_async_remote_copy(
        src_ref=sums_out, dst_ref=sums_out, send_sem=zs_sem.at[0], recv_sem=zr_sem.at[0, 0, 0],
        device_id=partner, device_id_type=MESH,
    ).wait_send()
    of_size(ids, 3, is_sem.at[0], ir_sem.at[0]).wait_send()
    of_size(ids, 28, is_sem.at[1], ir_sem.at[0]).wait_send()
    of_size(vals, REPS - 1, vs_sem.at[0], vr_sem.at[0]).wait_send()
    new_store.wait()
    upd_store.wait()


def hand_on(new_ref, upd_ref, new_out, upd_out, new_v, upd_v, load_sem, store_sem):
    loads, stores = [], []
    for n in range(8):
        held, src, dst = (new_v, new_ref.at[0], new_out.at[0]) if n < 4 else (upd_v, upd_ref, upd_out)
        at = pl.ds((n % 4) * SPAN, SPAN)
        loads.append(pltpu.make_async_copy(src.at[at], held.at[at], load_sem.at[n]))
        stores.append(pltpu.make_async_copy(held.at[at], dst.at[at], store_sem.at[n]))
        loads[n].start()
    for load, store in zip(loads, stores):
        load.wait()
        store.start()
    for store in stores:
        store.wait()


def local(inputs, up_grads, momentum, selected):
    lefts, rights = constants()
    hbm = pl.BlockSpec(memory_space=pl.ANY)
    sums = STREAMS * 2 * STREAM_ROWS
    new, upd = pl.pallas_call(
        kernel,
        out_shape=(
            jax.ShapeDtypeStruct((1, ROWS, COLS), F32),
            jax.ShapeDtypeStruct((ROWS, COLS), BF16),
        ),
        in_specs=[hbm] * 6,
        out_specs=(hbm, hbm),
        scratch_shapes=[
            pltpu.VMEM((1, 4, 8, 32), jnp.int32),
            pltpu.VMEM(lefts.shape, BF16),
            pltpu.VMEM(rights.shape, BF16),
            pltpu.VMEM((RING, 2, TOK, ROWS), BF16),
            pltpu.VMEM((RING, 2, ROWS, TOK), BF16),
            pltpu.VMEM((RING, FIRST * SPAN, TOK), BF16),
            pltpu.VMEM((TOK, COLS), BF16),
            pltpu.VMEM((TOK, COLS), BF16),
            pltpu.VMEM((ROWS, COLS), F32),
            pltpu.VMEM((sums, COLS), BF16),
            pltpu.VMEM((sums, COLS), BF16),
            pltpu.VMEM((SPAN, COLS), BF16),
            pltpu.VMEM((SPAN, COLS), BF16),
                pltpu.VMEM((ROWS, COLS), F32),
            pltpu.VMEM((ROWS, COLS), F32),
            pltpu.VMEM((ROWS, COLS), F32),
            pltpu.VMEM((REPS, LISTS, 128), jnp.int32),
            pltpu.VMEM((REPS, LISTS, 128), F32),
            pltpu.VMEM((LISTS, SPAN, REPS * 128), BF16),
            pltpu.VMEM((LISTS, REPS * 128, HALF), BF16),
            pltpu.VMEM((LISTS, HALF, 128), BF16),
            pltpu.VMEM((LISTS, SPAN, HALF), F32),
            pltpu.VMEM((ROWS, COLS), F32),
            pltpu.VMEM((ROWS, COLS), BF16),
            pltpu.SemaphoreType.DMA((21,)),
            pltpu.SemaphoreType.DMA((10,)),
            pltpu.SemaphoreType.DMA((10,)),
            pltpu.SemaphoreType.DMA((1,)),
            pltpu.SemaphoreType.DMA((2, STREAMS, 4)),
            pltpu.SemaphoreType.DMA((2,)),
            pltpu.SemaphoreType.DMA((len(AROUND),)),
            pltpu.SemaphoreType.DMA((1,)),
            pltpu.SemaphoreType.DMA((REPS // GROUP,)),
            pltpu.SemaphoreType.DMA((2,)),
        ],
        compiler_params=pltpu.CompilerParams(
            collective_id=0, has_side_effects=True, vmem_limit_bytes=56 * 1024 * 1024
        ),
        cost_estimate=pl.CostEstimate(flops=4 * 10**9, bytes_accessed=8 * 10**6, transcendentals=0),
    )(inputs, up_grads, momentum, selected, jnp.asarray(lefts), jnp.asarray(rights))
    return pl.pallas_call(
        hand_on,
        out_shape=(jax.ShapeDtypeStruct((1, ROWS, COLS), F32), jax.ShapeDtypeStruct((ROWS, COLS), BF16)),
        in_specs=[hbm, hbm],
        out_specs=(hbm, hbm),
        scratch_shapes=[
            pltpu.VMEM((ROWS, COLS), F32),
            pltpu.VMEM((ROWS, COLS), BF16),
            pltpu.SemaphoreType.DMA((8,)),
            pltpu.SemaphoreType.DMA((8,)),
        ],
    )(new, upd)


def solution(mesh):
    placed = (
        P("rep", "fsdp", None),
        P("rep", "fsdp", None),
        P("rep", "fsdp", None),
        P("rep", "fsdp", None, None),
    )
    return jax.shard_map(
        local,
        mesh=mesh,
        in_specs=placed,
        out_specs=(P("rep", "fsdp", None), P("fsdp", None)),
        check_vma=False,
    )
```

```python
import jax
import jax.numpy as jnp
import numpy as np
from jax import lax
from jax.experimental import pallas as pl
from jax.experimental.pallas import tpu as pltpu
from jax.sharding import PartitionSpec as P

MESH = pl.DeviceIdType.MESH
F32, BF16 = jnp.float32, jnp.bfloat16
SPAN, ROWS, COLS, TOK, RING, REPS = 64, 256, 512, 256, 8, 32
HALF = COLS // 2
AROUND = (0, 4, 3, 5, 2, 6, 1, 7)
GROUP = 8
LISTS = 8
decay, epsilon = 0.999, 1e-06
FIRST = 3
STREAMS = 5
STREAM_ROWS = 32 + 3 * SPAN


def split(x):
    hi = x.astype(BF16)
    return hi, (x - hi.astype(F32)).astype(BF16)


def constants():
    freq = np.arange(SPAN, dtype=np.float64)[:, None]
    sample = np.arange(SPAN, dtype=np.float64)[None, :]
    basis = np.cos(np.pi * (2.0 * sample + 1.0) * freq / (2.0 * SPAN))
    basis = basis * np.where(freq == 0, np.sqrt(1.0 / SPAN), np.sqrt(2.0 / SPAN))
    hi = basis.astype(BF16)
    lo = (basis - hi.astype(np.float64)).astype(BF16)

    def left(a, b):
        return np.concatenate([a, a, b, b], axis=1)

    def right(a):
        return np.kron(np.eye(4), a.astype(np.float64)).astype(BF16)

    lefts = np.stack([left(hi, lo), left(hi.T, lo.T)])
    rights = np.stack([right(hi.T), right(lo.T), right(hi), right(lo), right(np.ones((SPAN, SPAN)))])
    return lefts, rights


def dot(a, b):
    return jnp.dot(a, b, preferred_element_type=F32)


def dot_lanes(a, b):
    return lax.dot_general(a, b, (((1,), (1,)), ((), ())), preferred_element_type=F32)


def from_left(const, x):
    hi, lo = split(x)
    return dot(const, jnp.concatenate([hi, lo, hi, lo], axis=0))


def from_right(x, const_hi, const_lo):
    hi, lo = split(x)
    both = dot(jnp.concatenate([hi, lo], axis=0), const_hi)
    return both[: x.shape[0]] + both[x.shape[0] :] + dot(hi, const_lo)


def offset(way, stream, step):
    return (way * STREAMS + stream) * STREAM_ROWS + (0 if step == 0 else 32 + SPAN * (step - 1))


def kernel(
    x_hbm, g_hbm, m_hbm, sel_hbm, left_hbm, right_hbm, new_hbm, upd_hbm,
    sel_ref, left_ref, right_ref, x_in, xt, x_got, g_own, g_got, mom, sums_out, sums_in, b_out, b_in, grad, coef, mask,
    ids, vals, l_hot, r_hot, r_own, total, new_v, upd_v,
    load_sem, xs_sem, xr_sem, zs_sem, zr_sem, is_sem, ir_sem, vs_sem, vr_sem, out_sem,
):
    rep, fsdp = lax.axis_index("rep"), lax.axis_index("fsdp")
    core, y, x_lo = rep % 2, (rep // 2) % 8, rep // 16
    z, x_hi = fsdp // 2, fsdp % 2
    partner = (rep, z * 2 + 1 - x_hi)
    ways = [(rep, ((z + 1) % RING) * 2 + x_hi), (rep, ((z + RING - 1) % RING) * 2 + x_hi)]
    def there(dy, dx, dc):
        return (((x_lo + dx) % 2) * 16 + ((y + dy) % 8) * 2 + (core + dc) % 2, fsdp)

    around = [(dy, dx, dc) for dy in AROUND for dx in (0, 1) for dc in (0, 1)]
    near = [there(*d) for d in around[1:4]]
    far = {dy: there(dy, 0, 0) for dy in AROUND[1:]}

    order = (4, 3, 5, 2, 6, 1, 7, 0)
    x_loads = {}

    def load_x(dz, kind):
        column = ((z + dz) % RING) * 512 + (x_hi if kind == 0 else 1 - x_hi) * 256
        x_loads[dz, kind] = pltpu.make_async_copy(
            x_hbm.at[0, :, pl.ds(pl.multiple_of(column, 256), 256)], x_in.at[dz, kind], load_sem.at[2 * dz + kind]
        )
        x_loads[dz, kind].start()

    sel_load = pltpu.make_async_copy(sel_hbm, sel_ref, load_sem.at[16])
    g_load = pltpu.make_async_copy(g_hbm.at[0], g_own, load_sem.at[17])
    sel_load.start()
    load_x(4, 1)
    load_x(4, 0)
    g_load.start()

    barrier = pltpu.get_barrier_semaphore()
    for device in [partner, *ways, *(there(*d) for d in around[1:])]:
        pl.semaphore_signal(barrier, inc=1, device_id=device, device_id_type=MESH)

    for dz in order[1:]:
        load_x(dz, 1)
        load_x(dz, 0)
    m_load = pltpu.make_async_copy(m_hbm.at[0], mom, load_sem.at[18])
    left_load = pltpu.make_async_copy(left_hbm, left_ref, load_sem.at[19])
    right_load = pltpu.make_async_copy(right_hbm, right_ref, load_sem.at[20])
    for cp in (m_load, left_load, right_load):
        cp.start()

    sel_load.wait()
    rows = []
    for a in range(4):
        for h in range(2):
            rows.append(jnp.concatenate([sel_ref[0, a, 4 * h + j : 4 * h + j + 1, :] for j in range(4)], axis=1))
    own_ids = jnp.concatenate(rows, axis=0)
    ids[0] = own_ids

    pl.semaphore_wait(barrier, 3 + REPS - 1)

    def remote(src, dst, send_sem, recv_sem, device):
        cp = pltpu.make_async_remote_copy(
            src_ref=src, dst_ref=dst, send_sem=send_sem, recv_sem=recv_sem, device_id=device, device_id_type=MESH
        )
        cp.start()
        return cp

    x_sends = {}

    def turn(*distances):
        for dz in distances:
            for kind in (1, 0):
                x_loads[dz, kind].wait()
                xt[dz, kind] = x_in[dz, kind].T
                if kind == 1:
                    x_sends[dz] = remote(
                        xt.at[dz, 1, pl.ds(0, FIRST * SPAN)], x_got.at[dz], xs_sem.at[dz], xr_sem.at[dz], partner
                    )

    def wait_x(dz):
        x_sends[dz].wait_recv()

    def product(stream, dz):
        if stream < FIRST:
            at = pl.ds(stream * SPAN, SPAN)
            return dot(xt[dz, 0, at], g_own[...]) + dot(x_got[dz, at], g_got[...])
        return dot(xt[dz, 0 if stream == 3 else 1, pl.ds(FIRST * SPAN, SPAN)], g_own[...])

    z_copies = {}

    def send_sum(way, stream, step):
        size = 32 if step == 0 else SPAN
        at = pl.ds(offset(way, stream, step), size)
        z_copies[way, stream, step] = remote(
            sums_out.at[at], sums_in.at[at], zs_sem.at[0], zr_sem.at[way, stream, step], ways[way]
        )

    def arrived(way, stream, step):
        z_copies[way, stream, step].wait_recv()
        size = 32 if step == 0 else SPAN
        return sums_in[pl.ds(offset(way, stream, step), size), :].astype(F32)

    def chain(stream, step):
        if step == 0:
            term = product(stream, 4).astype(BF16)
            for way in range(2):
                sums_out[pl.ds(offset(way, stream, 0), 32), :] = term[32 * way : 32 * way + 32]
                send_sum(way, stream, 0)
            return
        terms = [product(stream, 4 - step), product(stream, 4 + step)]
        for way in range(2):
            term = terms[way]
            got = arrived(way, stream, step - 1)
            at = offset(way, stream, step)
            if step == 1:
                for part_ in range(2):
                    piece = term[32 * part_ : 32 * part_ + 32]
                    piece = piece + got if part_ == way else piece
                    sums_out[pl.ds(at + 32 * part_, 32), :] = piece.astype(BF16)
            else:
                sums_out[pl.ds(at, SPAN), :] = (term + got).astype(BF16)
            send_sum(way, stream, step)

    def finish(stream):
        return product(stream, 0) + arrived(0, stream, 3) + arrived(1, stream, 3)

    lane = lax.broadcasted_iota(jnp.int32, (1, 128), 1)
    count_u = lax.broadcasted_iota(jnp.int32, (SPAN, 128), 0)
    count_n = lax.broadcasted_iota(jnp.int32, (HALF, 128), 0)

    def hot(row):
        by_row = (row >> 6) == count_u
        by_column = (row & 63) + (lane >> 5) * SPAN == count_n
        return by_row.astype(F32).astype(BF16), by_column.astype(F32).astype(BF16)

    def send_near():
        for n, device in enumerate(near):
            remote(ids.at[0], ids.at[1 + n], is_sem.at[0], ir_sem.at[0], device)

    def send_far():
        landed(0)
        for dy, device in far.items():
            n = AROUND.index(8 - dy)
            remote(ids.at[pl.ds(0, 4)], ids.at[pl.ds(4 * n, 4)], is_sem.at[1], ir_sem.at[n], device)

    def of_size(slots, count, send_sem, recv_sem):
        at = slots.at[pl.ds(0, count)]
        return pltpu.make_async_remote_copy(
            src_ref=at, dst_ref=at, send_sem=send_sem, recv_sem=recv_sem, device_id=partner, device_id_type=MESH
        )

    def landed(n):
        of_size(ids, 3 if n == 0 else 4, is_sem.at[0], ir_sem.at[n]).wait_recv()

    def build(first, count):
        def one(r, carry):
            at = pl.ds(pl.multiple_of(r * 128, 128), 128)
            for s in range(LISTS):
                l, n = hot(ids[r, s : s + 1, :])
                l_hot[s, :, at] = l
                r_hot[s, at, :] = n.T
            return carry

        lax.fori_loop(first, first + count, one, 0)

    def own_mask():
        for s in range(LISTS):
            l, n = hot(own_ids[s : s + 1])
            r_own[s] = n
            a, h = s // 2, s % 2
            mask[pl.ds(a * SPAN, SPAN), pl.ds(h * HALF, HALF)] = dot_lanes(l, n)

    def transform(a):
        at = pl.ds(a * SPAN, SPAN)
        stepped = decay * mom[at, :] + grad[at, :]
        grad[at, :] = stepped
        partly = from_left(left_ref[0], stepped)
        kept = []
        for h in range(2):
            c = from_right(partly[:, h * HALF : (h + 1) * HALF], right_ref[0], right_ref[1])
            coef[at, pl.ds(h * HALF, HALF)] = c
            s = 2 * a + h
            hi, lo = split(c)
            both = dot(jnp.concatenate([hi, lo], axis=0), r_own[s])
            by_row = (own_ids[s : s + 1] >> 6) == count_u
            kept.append(jnp.sum(jnp.where(by_row, both[:SPAN] + both[SPAN:], 0.0), axis=0, keepdims=True))
        vals[0, pl.ds(2 * a, 2)] = jnp.concatenate(kept, axis=0)

    send_near()
    g_send = remote(g_hbm.at[0], g_got, xs_sem.at[8], xr_sem.at[8], partner)
    turn(4)
    g_load.wait()
    chain(3, 0)
    chain(4, 0)
    turn(3, 5)
    send_far()
    chain(3, 1)
    chain(4, 1)
    turn(2, 6)
    chain(3, 2)
    chain(4, 2)
    turn(1, 7)
    g_send.wait_recv()
    wait_x(4)
    for s in range(FIRST):
        chain(s, 0)
    chain(4, 3)
    chain(3, 3)
    turn(0)
    own_mask()
    build(0, 4)
    wait_x(3)
    wait_x(5)
    chain(0, 1)
    for n in range(1, 8):
        landed(n)
    build(4, 3)
    chain(1, 1)
    build(7, 3)
    chain(2, 1)
    build(10, 2)
    wait_x(2)
    wait_x(6)
    for s in range(FIRST):
        chain(s, 2)
        build(12 + 3 * s, 3)
    b_out[...] = finish(4).astype(BF16)
    b_send = remote(b_out, b_in, xs_sem.at[9], xr_sem.at[9], partner)
    wait_x(1)
    wait_x(7)
    for s in range(FIRST):
        chain(s, 3)
        build(21 + 3 * s, 3)
    build(30, 2)
    m_load.wait()
    left_load.wait()
    right_load.wait()
    own = finish(3)
    b_send.wait_recv()
    grad[pl.ds(FIRST * SPAN, SPAN), :] = own + b_in[...].astype(F32)
    transform(3)
    wait_x(0)
    for s in range(FIRST):
        grad[pl.ds(s * SPAN, SPAN), :] = finish(s)
        transform(s)

    for dy, dx, dc in around[1:]:
        slot = around.index(((8 - dy) % 8, dx, dc))
        remote(vals.at[0], vals.at[slot], vs_sem.at[0], vr_sem.at[slot // GROUP], there(dy, dx, dc))
    for a in range(4):
        at = pl.ds(a * SPAN, SPAN)
        partly = from_left(left_ref[1], coef[at, :] * mask[at, :])
        for h in range(2):
            cols = pl.ds(h * HALF, HALF)
            own = from_right(partly[:, h * HALF : (h + 1) * HALF], right_ref[2], right_ref[3])
            new_v[at, cols] = grad[at, cols] - own
    new_store = pltpu.make_async_copy(new_v, new_hbm.at[0], out_sem.at[0])
    new_store.start()

    for group in range(REPS // GROUP):
        of_size(vals, GROUP - (group == 0), vs_sem.at[0], vr_sem.at[group]).wait_recv()
        first, last = group * GROUP, (group + 1) * GROUP
        for s in range(LISTS):
            weighted = jnp.concatenate(
                [l_hot[s, :, r * 128 : (r + 1) * 128] * vals[r, s : s + 1, :].astype(BF16) for r in range(first, last)],
                axis=1,
            )
            term = dot(weighted, r_hot[s, pl.ds(first * 128, GROUP * 128)])
            total[s] = term if group == 0 else total[s] + term
    power = jnp.concatenate([jnp.sum(total[s] * total[s], axis=0, keepdims=True) for s in range(LISTS)], axis=0)
    hi, lo = split(power)
    power = dot(hi, right_ref[4]) + dot(lo, right_ref[4])
    scale = lax.rsqrt(power * (1.0 / (SPAN * SPAN)) + epsilon)
    for s in range(LISTS):
        decoded = from_right(from_left(left_ref[1], total[s]), right_ref[2], right_ref[3])
        at = (pl.ds((s // 2) * SPAN, SPAN), pl.ds((s % 2) * HALF, HALF))
        upd_v[at] = (decoded * scale[s : s + 1]).astype(BF16)
    upd_store = pltpu.make_async_copy(upd_v, upd_hbm, out_sem.at[1])
    upd_store.start()

    g_send.wait_send()
    for cp in x_sends.values():
        cp.wait_send()
    b_send.wait_send()
    pltpu.make_async_remote_copy(
        src_ref=sums_out, dst_ref=sums_out, send_sem=zs_sem.at[0], recv_sem=zr_sem.at[0, 0, 0],
        device_id=partner, device_id_type=MESH,
    ).wait_send()
    of_size(ids, 3, is_sem.at[0], ir_sem.at[0]).wait_send()
    of_size(ids, 28, is_sem.at[1], ir_sem.at[0]).wait_send()
    of_size(vals, REPS - 1, vs_sem.at[0], vr_sem.at[0]).wait_send()
    new_store.wait()
    upd_store.wait()


def hand_on(new_ref, upd_ref, new_out, upd_out, new_v, upd_v, load_sem, store_sem):
    loads, stores = [], []
    for n in range(8):
        held, src, dst = (new_v, new_ref.at[0], new_out.at[0]) if n < 4 else (upd_v, upd_ref, upd_out)
        at = pl.ds((n % 4) * SPAN, SPAN)
        loads.append(pltpu.make_async_copy(src.at[at], held.at[at], load_sem.at[n]))
        stores.append(pltpu.make_async_copy(held.at[at], dst.at[at], store_sem.at[n]))
        loads[n].start()
    for load, store in zip(loads, stores):
        load.wait()
        store.start()
    for store in stores:
        store.wait()


def local(inputs, up_grads, momentum, selected):
    lefts, rights = constants()
    hbm = pl.BlockSpec(memory_space=pl.ANY)
    sums = STREAMS * 2 * STREAM_ROWS
    new, upd = pl.pallas_call(
        kernel,
        out_shape=(
            jax.ShapeDtypeStruct((1, ROWS, COLS), F32),
            jax.ShapeDtypeStruct((ROWS, COLS), BF16),
        ),
        in_specs=[hbm] * 6,
        out_specs=(hbm, hbm),
        scratch_shapes=[
            pltpu.VMEM((1, 4, 8, 32), jnp.int32),
            pltpu.VMEM(lefts.shape, BF16),
            pltpu.VMEM(rights.shape, BF16),
            pltpu.VMEM((RING, 2, TOK, ROWS), BF16),
            pltpu.VMEM((RING, 2, ROWS, TOK), BF16),
            pltpu.VMEM((RING, FIRST * SPAN, TOK), BF16),
            pltpu.VMEM((TOK, COLS), BF16),
            pltpu.VMEM((TOK, COLS), BF16),
            pltpu.VMEM((ROWS, COLS), F32),
            pltpu.VMEM((sums, COLS), BF16),
            pltpu.VMEM((sums, COLS), BF16),
            pltpu.VMEM((SPAN, COLS), BF16),
            pltpu.VMEM((SPAN, COLS), BF16),
                pltpu.VMEM((ROWS, COLS), F32),
            pltpu.VMEM((ROWS, COLS), F32),
            pltpu.VMEM((ROWS, COLS), F32),
            pltpu.VMEM((REPS, LISTS, 128), jnp.int32),
            pltpu.VMEM((REPS, LISTS, 128), F32),
            pltpu.VMEM((LISTS, SPAN, REPS * 128), BF16),
            pltpu.VMEM((LISTS, REPS * 128, HALF), BF16),
            pltpu.VMEM((LISTS, HALF, 128), BF16),
            pltpu.VMEM((LISTS, SPAN, HALF), F32),
            pltpu.VMEM((ROWS, COLS), F32),
            pltpu.VMEM((ROWS, COLS), BF16),
            pltpu.SemaphoreType.DMA((21,)),
            pltpu.SemaphoreType.DMA((10,)),
            pltpu.SemaphoreType.DMA((10,)),
            pltpu.SemaphoreType.DMA((1,)),
            pltpu.SemaphoreType.DMA((2, STREAMS, 4)),
            pltpu.SemaphoreType.DMA((2,)),
            pltpu.SemaphoreType.DMA((len(AROUND),)),
            pltpu.SemaphoreType.DMA((1,)),
            pltpu.SemaphoreType.DMA((REPS // GROUP,)),
            pltpu.SemaphoreType.DMA((2,)),
        ],
        compiler_params=pltpu.CompilerParams(
            collective_id=0, has_side_effects=True, vmem_limit_bytes=56 * 1024 * 1024
        ),
        cost_estimate=pl.CostEstimate(flops=4 * 10**9, bytes_accessed=8 * 10**6, transcendentals=0),
    )(inputs, up_grads, momentum, selected, jnp.asarray(lefts), jnp.asarray(rights))
    return pl.pallas_call(
        hand_on,
        out_shape=(jax.ShapeDtypeStruct((1, ROWS, COLS), F32), jax.ShapeDtypeStruct((ROWS, COLS), BF16)),
        in_specs=[hbm, hbm],
        out_specs=(hbm, hbm),
        scratch_shapes=[
            pltpu.VMEM((ROWS, COLS), F32),
            pltpu.VMEM((ROWS, COLS), BF16),
            pltpu.SemaphoreType.DMA((8,)),
            pltpu.SemaphoreType.DMA((8,)),
        ],
    )(new, upd)


def solution(mesh):
    placed = (
        P("rep", "fsdp", None),
        P("rep", "fsdp", None),
        P("rep", "fsdp", None),
        P("rep", "fsdp", None, None),
    )
    return jax.shard_map(
        local,
        mesh=mesh,
        in_specs=placed,
        out_specs=(P("rep", "fsdp", None), P("fsdp", None)),
        check_vma=False,
    )
```
